256 devices in a mesh: blk: 128 (over y, x, z_lo, core), rep: 2 (over z_hi).
Axes of the slice: x: 4, y: 4, z: 8 (z_hi: 2, z_lo: 4; z = z_hi * 4 + z_lo), core: 2. Of those that a mesh axis runs over, the one named last changes fastest.
Arguments:
- tracks: bfloat16 [131072, 512], P(('blk', 'rep')), may hold values from -80 to 80
Outputs:
- neighbour_sums: bfloat16 [131072, 512], P(('blk', 'rep'))
The draws below stay inside these ranges and needn't reach their ends.
All inputs are finite; a program needn't handle non-finite values.
Results may differ from the reference program's by a relative error of at most 0.0071.
Values may be sent and summed in bfloat16 or wider, within the bound.
A program may use at most 64 MiB of HBM per device.

```python
import math
import jax
import jax.numpy as jnp
from jax import lax

F = 512
R_DEV = 512
STEPS = 3
NS_ITERS = 4
INV_TEMP = 2
TRACKS = 131072
N_BLK = 128
N_REP = 2


def draw_tracks(key, part):
    key = jax.random.fold_in(key, 1)
    keys = jax.random.split(key, 6)
    columns = jnp.exp(jax.random.uniform(keys[1], (F,), jnp.float32) * jnp.log(4.0))
    rising = jnp.exp(jnp.log(3.0) * jnp.arange(TRACKS, dtype=jnp.float32) / TRACKS)
    jitter = jnp.exp(jax.random.uniform(keys[2], (TRACKS,), jnp.float32, -0.35, 0.35))
    base = jax.random.normal(keys[0], (TRACKS, F), jnp.float32)
    values = base * columns[None, :] * (rising * jitter)[:, None]
    level = 10.0 * (32.0 / F) ** 0.25
    blocks = values.reshape(TRACKS // 256, 256, F)
    anchor = jnp.clip(jax.random.uniform(keys[5], (TRACKS // 256, F), jnp.float32, -1.7, 1.7), -1.5, 1.5) * columns[None, :]
    noise = 0.05 * jax.random.normal(keys[4], (TRACKS // 256, 3, F), jnp.float32) * columns[None, None, :]
    levels = jnp.array([level, level, 0.85 * level], jnp.float32)
    planted = levels[None, :, None] * anchor[:, None, :] + noise
    blocks = blocks.at[:, 0:3].set(planted)
    values = blocks.reshape(TRACKS, F)
    return jnp.clip(values, -80.0, 80.0).astype(jnp.bfloat16)


def setup_inputs(seed: int = 0) -> dict:
    key_list = jax.random.split(jax.random.key(seed), 2)
    return {
        "tracks": draw_tracks(jax.random.fold_in(key_list[1], 71), 0),
    }


EPSILON = 1e-05

def inverse_root(covariance):
    width = covariance.shape[0]
    identity = jnp.eye(width, dtype=covariance.dtype)
    shifted = covariance + EPSILON * identity
    frobenius = jnp.sqrt(jnp.sum(shifted * shifted))
    iterate = shifted / frobenius
    inverse = identity
    for sweep in range(NS_ITERS):
        factor = 1.5 * identity - 0.5 * jnp.dot(inverse, iterate, precision=lax.Precision.HIGHEST)
        iterate = jnp.dot(iterate, factor, precision=lax.Precision.HIGHEST)
        inverse = jnp.dot(factor, inverse, precision=lax.Precision.HIGHEST)
    return inverse / jnp.sqrt(frobenius)

def reference(tracks):
    values = tracks.astype(jnp.float32)
    average = lax.optimization_barrier(jnp.sum(values, axis=0)) / TRACKS
    centred = values - average
    covariance = jnp.dot(centred.T, centred, precision=lax.Precision.HIGHEST) / TRACKS
    whitener = inverse_root(covariance)
    whitened = jnp.dot(centred, whitener, precision=lax.Precision.HIGHEST).astype(jnp.bfloat16)
    group_size = R_DEV * N_REP
    span = STEPS * N_REP
    grouped = whitened.reshape(N_BLK, group_size, F)
    score_scale = INV_TEMP / math.sqrt(F)

    def one_group(index):
        queries = lax.dynamic_index_in_dim(grouped, index, 0, keepdims=False)
        picks = ((index - jnp.arange(span, dtype=jnp.int32)) % N_BLK).astype(jnp.int32)
        key_rows = jnp.take(grouped, picks, axis=0).reshape(span * group_size, F)
        scores = lax.dot_general(queries, key_rows, (((1,), (1,)), ((), ())), preferred_element_type=jnp.float32) * score_scale
        itself = jnp.arange(group_size)[:, None] == jnp.arange(span * group_size)[None, :]
        scores = jnp.where(itself, -jnp.inf, scores)
        highest = lax.optimization_barrier(jnp.max(scores, axis=1))
        expo = jnp.exp(scores - highest[:, None])
        totals = lax.optimization_barrier(jnp.sum(expo, axis=1))
        numer = jnp.dot(expo.astype(jnp.bfloat16), key_rows, preferred_element_type=jnp.float32)
        return (numer / totals[:, None]).astype(jnp.bfloat16)
    result_rows = lax.map(one_group, jnp.arange(N_BLK, dtype=jnp.int32))
    return result_rows.reshape(TRACKS, F)
```

```python
import functools
import math

import jax
import jax.numpy as jnp
from jax import lax
from jax.experimental import pallas as pl
from jax.experimental.pallas import tpu as pltpu
from jax.sharding import PartitionSpec as P

NS_ITERS = 4
INV_TEMP = 2
EPSILON = 1e-05
WIDTH = 512
ROWS = 512
TRACKS = 131072
MESH = pl.DeviceIdType.MESH
F32 = jnp.float32
BF16 = jnp.bfloat16

TILES = [(i, j) for i in range(4) for j in range(i, 4)]
HALF = 640
PART = 40
PLANE = [(dy, dx) for dy in range(4) for dx in range(4)][1:]

OWN, BACK, RING, SIDE, MATE, MATE_RING = 0, 0, 4, 8, 12, 15
SLOTS = 18
CHUNKS = 2
CHUNK = ROWS // CHUNKS


def place(y, x, z, core):
    return (((y * 4 + x) * 4 + z % 4) * 2 + core, z // 4)


def split(value):
    high = value.astype(BF16)
    return high, (value - high.astype(F32)).astype(BF16)


def dot(left, right):
    return jnp.dot(left, right, preferred_element_type=F32)


def product(left, right):
    return dot(left[0], right[0]) + (dot(left[0], right[1]) + dot(left[1], right[0]))


def kernel(
    tracks_ref, out_ref, keys, halves, from_mate, outgoing, plane_in, line_out, line_in, full,
    iterate, inverse, scores, weighted, queries, whitener, load_sem, ring_send, ring_recv,
    back_send, back_recv, side_send, side_recv, mate_send, mate_recv, core_send, core_recv,
    plane_send, plane_recv, line_send, line_recv, gather_send, gather_recv, whole_send, whole_recv,
):
    group = lax.axis_index("blk")
    rep = lax.axis_index("rep")
    y, x, core = group // 32, (group // 8) % 4, group % 2
    step_z = (group // 2) % 4
    z = rep * 4 + step_z
    mine = y * 4 + x
    wrap = (x + 1) // 4
    next_y, next_x = (y + wrap) % 4, (x + 1) % 4
    back_wrap = (4 - x) // 4
    last_y, last_x = (y + 3 * back_wrap) % 4, (x + 3) % 4
    mate = place(y, x, z, 1 - core)
    down = place(y, x, (z + 7) % 8, core)
    column = place(next_y, next_x, z, core)
    at_end = (step_z + 1) // 4
    at_start = (4 - step_z) // 4
    ahead = place(
        at_end * next_y + (1 - at_end) * y, at_end * next_x + (1 - at_end) * x, (z + 1) % 8, core
    )
    behind = place(
        at_start * last_y + (1 - at_start) * y,
        at_start * last_x + (1 - at_start) * x,
        (z + 7) % 8,
        core,
    )

    load = pltpu.make_async_copy(tracks_ref, keys.at[OWN], load_sem)
    load.start()
    barrier = pltpu.get_barrier_semaphore()

    def greet(device):
        pl.semaphore_signal(barrier, inc=1, device_id=device, device_id_type=MESH)

    greet(mate)
    for dz in range(1, 8):
        greet(place(y, x, (z + dz) % 8, core))
    for dy, dx in PLANE:
        greet(place((y + dy) % 4, (x + dx) % 4, z, core))

    @pl.when(at_end == 1)
    def _():
        greet(ahead)

    @pl.when(at_start == 1)
    def _():
        greet(behind)

    load.wait()

    rows = keys[OWN]
    gram = lax.dot_general(rows, rows, (((0,), (0,)), ((), ())), preferred_element_type=F32)
    for n, (i, j) in enumerate(TILES):
        halves[n // 5, pl.ds(128 * (n % 5), 128), :] = gram[
            128 * i : 128 * (i + 1), 128 * j : 128 * (j + 1)
        ]
    sums = jnp.sum(rows.astype(F32), axis=0, keepdims=True)
    tail = jnp.concatenate(
        [sums[:, 128 * i : 128 * (i + 1)] for i in range(4)] + [jnp.zeros((4, 128), F32)], axis=0
    )
    for h in range(2):
        halves[h, pl.ds(HALF, 8), :] = tail

    pl.semaphore_wait(barrier, 23 + at_end + at_start)

    def piece(slot, part):
        return keys.at[slot, pl.ds(part * CHUNK, CHUNK)]

    def mover(source, target, part, send, recv, device):
        return pltpu.make_async_remote_copy(
            src_ref=piece(source, part),
            dst_ref=piece(target, part),
            send_sem=send,
            recv_sem=recv,
            device_id=device,
            device_id_type=MESH,
        )

    def ring_hop(s, part):
        source = OWN if s == 3 else RING + s + 1
        return mover(
            source, RING + s, part, ring_send.at[s, part], ring_recv.at[s, part], down
        )

    def back_hop(s, part):
        return mover(
            BACK + s - 1, BACK + s, part, back_send.at[s, part], back_recv.at[s, part], ahead
        )

    def side_hop(s, part):
        return mover(
            RING + s, SIDE + s, part, side_send.at[s, part], side_recv.at[s, part], column
        )

    def used(s):
        return RING + s + 4 * jnp.minimum(jnp.maximum(s - step_z, 0), 1)

    def mate_back(i, part):
        return mover(
            BACK + core + i, MATE + i, part, mate_send.at[i, part], mate_recv.at[i, part], mate
        )

    def mate_ring(i, part):
        return mover(
            used(core + i), MATE_RING + i, part,
            mate_send.at[3 + i, part], mate_recv.at[3 + i, part], mate,
        )

    def each(act):
        for part in range(CHUNKS):
            act(part)

    def sides(s, act):
        cond = step_z < s
        if s == 3:
            cond = jnp.logical_and(cond, core == 1)

        @pl.when(cond)
        def _():
            act()

    def start_own():
        each(lambda part: ring_hop(3, part).start())
        each(lambda part: back_hop(1, part).start())

    def pass_ring(s, part):
        ring_hop(s, part).wait_recv()
        if s > 0:
            ring_hop(s - 1, part).start()
            sides(s, lambda: side_hop(s, part).start())

    def pass_back(s, part):
        back_hop(s, part).wait_recv()
        if s == 1:
            back_hop(2, part).start()
        if s == 2:

            @pl.when(core == 1)
            def _():
                back_hop(3, part).start()

    start_core = pltpu.make_async_remote_copy(
        src_ref=halves.at[1 - core], dst_ref=from_mate, send_sem=core_send, recv_sem=core_recv,
        device_id=mate, device_id_type=MESH,
    )
    start_core.start()
    start_own()
    start_core.wait_recv()
    chip = halves[core] + from_mate[...]
    for q in range(16):
        outgoing[q, pl.ds(0, PART), :] = chip[PART * q : PART * (q + 1)]
        outgoing[q, pl.ds(PART, 8), :] = chip[HALF : HALF + 8]

    def plane_hop(n, dy, dx):
        ty, tx = (y + dy) % 4, (x + dx) % 4
        return pltpu.make_async_remote_copy(
            src_ref=outgoing.at[ty * 4 + tx], dst_ref=plane_in.at[n], send_sem=plane_send,
            recv_sem=plane_recv, device_id=place(ty, tx, z, core), device_id_type=MESH,
        )

    for n, (dy, dx) in enumerate(PLANE):
        plane_hop(n, dy, dx).start()
    pltpu.make_async_copy(plane_in, plane_in, plane_recv).wait()
    line_out[...] = outgoing[mine] + jnp.sum(plane_in[...], axis=0)

    def line_hop(dz):
        return pltpu.make_async_remote_copy(
            src_ref=line_out, dst_ref=line_in.at[dz - 1], send_sem=line_send, recv_sem=line_recv,
            device_id=place(y, x, (z + dz) % 8, core), device_id_type=MESH,
        )

    for dz in range(1, 8):
        line_hop(dz).start()
    each(lambda part: pass_ring(3, part))
    each(lambda part: pass_back(1, part))
    pltpu.make_async_copy(line_in, line_in, line_recv).wait()
    total = line_out[...] + jnp.sum(line_in[...], axis=0)
    full[core, pl.ds(pl.multiple_of(PART * mine, 8), PART), :] = total[:PART]
    average = total[PART : PART + 4] / TRACKS

    def gather_hop(dy, dx):
        area = full.at[core, pl.ds(pl.multiple_of(PART * mine, 8), PART)]
        return pltpu.make_async_remote_copy(
            src_ref=area, dst_ref=area, send_sem=gather_send, recv_sem=gather_recv,
            device_id=place((y + dy) % 4, (x + dx) % 4, z, core), device_id_type=MESH,
        )

    for dy, dx in PLANE:
        gather_hop(dy, dx).start()
    each(lambda part: pass_ring(2, part))
    each(lambda part: pass_back(2, part))
    others = full.at[core, pl.ds(0, PART * 15)]
    pltpu.make_async_copy(others, others, gather_recv).wait()
    whole = pltpu.make_async_remote_copy(
        src_ref=full.at[core], dst_ref=full.at[core], send_sem=whole_send, recv_sem=whole_recv,
        device_id=mate, device_id_type=MESH,
    )
    whole.start()
    whole.wait()

    square = jnp.zeros((1, 1), F32)
    row_id = lax.broadcasted_iota(jnp.int32, (128, 128), 0)
    col_id = lax.broadcasted_iota(jnp.int32, (128, 128), 1)
    eye = (row_id == col_id).astype(F32)
    upright = [jnp.broadcast_to(average[i : i + 1], (128, 128)).T for i in range(4)]
    for n, (i, j) in enumerate(TILES):
        tile = full[n // 5, pl.ds(128 * (n % 5), 128), :] / TRACKS - upright[i] * average[j : j + 1]
        if i == j:
            tile = tile + EPSILON * eye
        part = jnp.sum(jnp.sum(tile * tile, axis=0, keepdims=True), axis=1, keepdims=True)
        square = square + (part if i == j else 2.0 * part)
        iterate[pl.ds(128 * i, 128), pl.ds(128 * j, 128)] = tile
        if i != j:
            iterate[pl.ds(128 * j, 128), pl.ds(128 * i, 128)] = tile.T
    frobenius = jnp.sqrt(square)
    iterate[...] = iterate[...] / frobenius

    full_row = lax.broadcasted_iota(jnp.int32, (WIDTH, WIDTH), 0)
    full_col = lax.broadcasted_iota(jnp.int32, (WIDTH, WIDTH), 1)
    diagonal = full_row == full_col

    def factor_of(matrix):
        return jnp.where(diagonal, 1.5, 0.0) - 0.5 * matrix

    for sweep in range(NS_ITERS - 1):
        factor = split(factor_of(iterate[...]))
        if sweep == 0:
            inverse[...] = factor_of(iterate[...])
        else:
            inverse[...] = product(split(inverse[...]), factor)
        iterate[...] = product(split(iterate[...]), split(product(factor, factor)))
        if sweep == 0:
            each(lambda part: pass_ring(1, part))
    unscaled = product(split(inverse[...]), split(factor_of(iterate[...])))
    whitener[...] = unscaled / jnp.sqrt(frobenius)
    weights = split(whitener[...])
    centre = jnp.concatenate([average[i : i + 1] for i in range(4)], axis=1)
    centred = keys[OWN].astype(F32) - centre
    turned = product(split(product(split(centred), weights)), weights)
    queries[...] = (turned * (INV_TEMP / math.sqrt(WIDTH) * math.log2(math.e))).astype(BF16)

    @pl.when(core == 1)
    def _():
        each(lambda part: back_hop(3, part).wait_recv())

    for i in range(3):
        each(lambda part: mate_back(i, part).start())
    for s in range(1, 4):
        sides(s, lambda: each(lambda part: side_hop(s, part).wait_recv()))
    each(lambda part: pass_ring(0, part))
    for i in range(3):
        each(lambda part: mate_ring(i, part).start())
    for i in range(3):
        each(lambda part: mate_back(i, part).wait_recv())
        each(lambda part: mate_ring(i, part).wait_recv())

    def key_slot(n):
        return jnp.where(n < 3, n, jnp.where(n < 6, used(n - 3), n + 6))

    def score(n, high):
        found = lax.dot_general(
            queries[...], keys[key_slot(n)], (((1,), (1,)), ((), ())), preferred_element_type=F32
        )
        found = jnp.where(jnp.logical_and(diagonal, n == 0), -jnp.inf, found)
        scores[n] = found
        for i in range(4):
            high = jnp.maximum(high, found[:, 128 * i : 128 * (i + 1)])
        return high

    high = lax.fori_loop(0, 12, score, jnp.full((ROWS, 128), -jnp.inf, F32))
    highest = jnp.max(high, axis=1, keepdims=True)
    weighted[...] = jnp.zeros_like(weighted)

    def spread(n, totals):
        weight = jnp.exp2(scores[n] - highest).astype(BF16)
        weighted[...] += dot(weight, keys[key_slot(n)])
        wide = weight.astype(F32)
        for i in range(4):
            totals = totals + wide[:, 128 * i : 128 * (i + 1)]
        return totals

    totals = lax.fori_loop(0, 12, spread, jnp.zeros((ROWS, 128), F32))
    totals = jnp.sum(totals, axis=1, keepdims=True)
    mixed = weighted[...] / totals - centre
    out_ref[...] = product(split(mixed), split(whitener[...])).astype(BF16)

    start_core.wait_send()
    pltpu.make_async_copy(plane_in, plane_in, plane_send).wait()
    pltpu.make_async_copy(line_in, line_in, line_send).wait()
    pltpu.make_async_copy(others, others, gather_send).wait()
    for part in range(CHUNKS):
        for s in range(4):
            ring_hop(s, part).wait_send()
        back_hop(1, part).wait_send()
        back_hop(2, part).wait_send()
        for i in range(3):
            mate_back(i, part).wait_send()
            mate_ring(i, part).wait_send()
    for s in range(1, 4):
        sides(s, lambda: each(lambda part: side_hop(s, part).wait_send()))

    @pl.when(core == 1)
    def _():
        each(lambda part: back_hop(3, part).wait_send())


def local(tracks):
    dma = pltpu.SemaphoreType.DMA
    return pl.pallas_call(
        kernel,
        out_shape=jax.ShapeDtypeStruct((ROWS, WIDTH), BF16),
        in_specs=[pl.BlockSpec(memory_space=pl.ANY)],
        out_specs=pl.BlockSpec(memory_space=pltpu.VMEM),
        scratch_shapes=[
            pltpu.VMEM((SLOTS, ROWS, WIDTH), BF16),
            pltpu.VMEM((2, HALF + 8, 128), F32),
            pltpu.VMEM((HALF + 8, 128), F32),
            pltpu.VMEM((16, PART + 8, 128), F32),
            pltpu.VMEM((15, PART + 8, 128), F32),
            pltpu.VMEM((PART + 8, 128), F32),
            pltpu.VMEM((7, PART + 8, 128), F32),
            pltpu.VMEM((2, HALF, 128), F32),
            pltpu.VMEM((WIDTH, WIDTH), F32),
            pltpu.VMEM((WIDTH, WIDTH), F32),
            pltpu.VMEM((12, ROWS, ROWS), F32),
            pltpu.VMEM((ROWS, WIDTH), F32),
            pltpu.VMEM((ROWS, WIDTH), BF16),
            pltpu.VMEM((WIDTH, WIDTH), F32),
            dma(()),
            dma((4, CHUNKS)), dma((4, CHUNKS)),
            dma((4, CHUNKS)), dma((4, CHUNKS)),
            dma((4, CHUNKS)), dma((4, CHUNKS)),
            dma((6, CHUNKS)), dma((6, CHUNKS)),
            dma(()), dma(()), dma(()), dma(()), dma(()), dma(()), dma(()), dma(()), dma(()), dma(()),
        ],
        compiler_params=pltpu.CompilerParams(
            collective_id=0, has_side_effects=True, vmem_limit_bytes=56 * 1024 * 1024
        ),
    )(tracks)


def solution(mesh):
    spec = P(("blk", "rep"), None)
    return jax.shard_map(local, mesh=mesh, in_specs=(spec,), out_specs=spec, check_vma=False)
```

```python
import functools
import math

import jax
import jax.numpy as jnp
from jax import lax
from jax.experimental import pallas as pl
from jax.experimental.pallas import tpu as pltpu
from jax.sharding import PartitionSpec as P

NS_ITERS = 4
INV_TEMP = 2
EPSILON = 1e-05
WIDTH = 512
ROWS = 512
TRACKS = 131072
MESH = pl.DeviceIdType.MESH
F32 = jnp.float32
BF16 = jnp.bfloat16

TILES = [(i, j) for i in range(4) for j in range(i, 4)]
HALF = 640
PART = 40
PLANE = [(dy, dx) for dy in range(4) for dx in range(4)][1:]

OWN, BACK, RING, SIDE, MATE, MATE_RING = 0, 0, 4, 8, 12, 15
SLOTS = 18
CHUNKS = 2
CHUNK = ROWS // CHUNKS


def place(y, x, z, core):
    return (((y * 4 + x) * 4 + z % 4) * 2 + core, z // 4)


def split(value):
    high = value.astype(BF16)
    return high, (value - high.astype(F32)).astype(BF16)


def dot(left, right):
    return jnp.dot(left, right, preferred_element_type=F32)


def product(left, right):
    return dot(left[0], right[0]) + (dot(left[0], right[1]) + dot(left[1], right[0]))


def kernel(
    tracks_ref, out_ref, keys, halves, from_mate, outgoing, plane_in, line_out, line_in, full,
    iterate, inverse, scores, weighted, queries, whitener, load_sem, ring_send, ring_recv,
    back_send, back_recv, side_send, side_recv, mate_send, mate_recv, core_send, core_recv,
    plane_send, plane_recv, line_send, line_recv, gather_send, gather_recv, whole_send, whole_recv,
):
    group = lax.axis_index("blk")
    rep = lax.axis_index("rep")
    y, x, core = group // 32, (group // 8) % 4, group % 2
    step_z = (group // 2) % 4
    z = rep * 4 + step_z
    mine = y * 4 + x
    wrap = (x + 1) // 4
    next_y, next_x = (y + wrap) % 4, (x + 1) % 4
    mate = place(y, x, z, 1 - core)
    down = place(y, x, (z + 7) % 8, core)
    column = place(next_y, next_x, z, core)
    up = place(y, x, (z + 1) % 8, core)
    at_end = (step_z + 1) // 4

    load = pltpu.make_async_copy(tracks_ref, keys.at[OWN], load_sem)
    load.start()
    barrier = pltpu.get_barrier_semaphore()

    def greet(device):
        pl.semaphore_signal(barrier, inc=1, device_id=device, device_id_type=MESH)

    greet(mate)
    for dz in range(1, 8):
        greet(place(y, x, (z + dz) % 8, core))
    for dy, dx in PLANE:
        greet(place((y + dy) % 4, (x + dx) % 4, z, core))

    load.wait()

    rows = keys[OWN]
    gram = lax.dot_general(rows, rows, (((0,), (0,)), ((), ())), preferred_element_type=F32)
    for n, (i, j) in enumerate(TILES):
        halves[n // 5, pl.ds(128 * (n % 5), 128), :] = gram[
            128 * i : 128 * (i + 1), 128 * j : 128 * (j + 1)
        ]
    sums = jnp.sum(rows.astype(F32), axis=0, keepdims=True)
    tail = jnp.concatenate(
        [sums[:, 128 * i : 128 * (i + 1)] for i in range(4)] + [jnp.zeros((4, 128), F32)], axis=0
    )
    for h in range(2):
        halves[h, pl.ds(HALF, 8), :] = tail

    pl.semaphore_wait(barrier, 23)

    def piece(slot, part):
        return keys.at[slot, pl.ds(part * CHUNK, CHUNK)]

    def mover(source, target, part, send, recv, device):
        return pltpu.make_async_remote_copy(
            src_ref=piece(source, part),
            dst_ref=piece(target, part),
            send_sem=send,
            recv_sem=recv,
            device_id=device,
            device_id_type=MESH,
        )

    def ring_hop(s, part):
        source = OWN if s == 3 else RING + s + 1
        return mover(
            source, RING + s, part, ring_send.at[s, part], ring_recv.at[s, part], down
        )

    def back_hop(s, part):
        source = BACK + s - 1 + at_end * (SIDE - BACK + 1)
        return mover(
            source, BACK + s, part, back_send.at[s, part], back_recv.at[s, part], up
        )

    def side_hop(s, part):
        source = RING + s + at_end * (BACK - 1 - RING)
        return mover(
            source, SIDE + s, part, side_send.at[s, part], side_recv.at[s, part], column
        )

    def used(s):
        return RING + s + 4 * jnp.minimum(jnp.maximum(s - step_z, 0), 1)

    def mate_back(i, part):
        return mover(
            BACK + core + i, MATE + i, part, mate_send.at[i, part], mate_recv.at[i, part], mate
        )

    def mate_ring(i, part):
        return mover(
            used(core + i), MATE_RING + i, part,
            mate_send.at[3 + i, part], mate_recv.at[3 + i, part], mate,
        )

    def each(act):
        for part in range(CHUNKS):
            act(part)

    def start_mate_back(i):
        each(lambda part: mate_back(i, part).start())

    def start_mate_ring(i):
        each(lambda part: mate_ring(i, part).start())

    def when(cond, act):
        @pl.when(cond)
        def _():
            act()

    inner = step_z < 3
    last = step_z == 3
    second = core == 1

    both = jnp.logical_and

    def lower(s):
        return both(step_z < s, second) if s == 3 else step_z < s

    def start_own(part):
        ring_hop(3, part).start()
        when(inner, lambda: back_hop(1, part).start())

    def take_ring(s, part):
        ring_hop(s, part).wait_recv()

    def send_ring(s, part):
        ring_hop(s - 1, part).start()

    def pass_ring(s, part):
        take_ring(s, part)
        send_ring(s, part)

    def drop(s, part):
        when(lower(s), lambda: side_hop(s, part).start())

    def lift(s, part):
        when(both(last, second) if s == 3 else last, lambda: side_hop(s, part).start())

    def pass_end(s, part):
        def go():
            side_hop(s, part).wait_recv()
            back_hop(s, part).start()

        when(both(last, second) if s == 3 else last, go)

    def pass_back(s, part, here):
        def go():
            back_hop(s, part).wait_recv()
            if s < 3:
                sends = both(inner, second) if s == 2 else inner
                when(sends, lambda: back_hop(s + 1, part).start())

        when(both(here, second) if s == 3 else here, go)

    def take_side(s, part):
        when(lower(s), lambda: side_hop(s, part).wait_recv())

    start_core = pltpu.make_async_remote_copy(
        src_ref=halves.at[1 - core], dst_ref=from_mate, send_sem=core_send, recv_sem=core_recv,
        device_id=mate, device_id_type=MESH,
    )
    start_core.start()
    each(start_own)
    start_core.wait_recv()
    chip = halves[core] + from_mate[...]
    for q in range(16):
        outgoing[q, pl.ds(0, PART), :] = chip[PART * q : PART * (q + 1)]
        outgoing[q, pl.ds(PART, 8), :] = chip[HALF : HALF + 8]

    def plane_hop(n, dy, dx):
        ty, tx = (y + dy) % 4, (x + dx) % 4
        return pltpu.make_async_remote_copy(
            src_ref=outgoing.at[ty * 4 + tx], dst_ref=plane_in.at[n], send_sem=plane_send,
            recv_sem=plane_recv, device_id=place(ty, tx, z, core), device_id_type=MESH,
        )

    for n, (dy, dx) in enumerate(PLANE):
        plane_hop(n, dy, dx).start()
    each(lambda part: lift(1, part))
    pltpu.make_async_copy(plane_in, plane_in, plane_recv).wait()
    line_out[...] = outgoing[mine] + jnp.sum(plane_in[...], axis=0)

    def line_hop(dz):
        return pltpu.make_async_remote_copy(
            src_ref=line_out, dst_ref=line_in.at[dz - 1], send_sem=line_send, recv_sem=line_recv,
            device_id=place(y, x, (z + dz) % 8, core), device_id_type=MESH,
        )

    for dz in range(1, 8):
        line_hop(dz).start()
    for part in range(CHUNKS):
        pass_back(1, part, last)
        lift(2, part)
        take_ring(3, part)
        drop(3, part)
    pltpu.make_async_copy(line_in, line_in, line_recv).wait()
    total = line_out[...] + jnp.sum(line_in[...], axis=0)
    full[core, pl.ds(pl.multiple_of(PART * mine, 8), PART), :] = total[:PART]
    average = total[PART : PART + 4] / TRACKS

    def gather_hop(dy, dx):
        area = full.at[core, pl.ds(pl.multiple_of(PART * mine, 8), PART)]
        return pltpu.make_async_remote_copy(
            src_ref=area, dst_ref=area, send_sem=gather_send, recv_sem=gather_recv,
            device_id=place((y + dy) % 4, (x + dx) % 4, z, core), device_id_type=MESH,
        )

    for dy, dx in PLANE:
        gather_hop(dy, dx).start()
    for part in range(CHUNKS):
        send_ring(3, part)
        pass_end(1, part)
        pass_back(1, part, both(step_z > 0, inner))
    each(lambda part: pass_end(2, part))
    others = full.at[core, pl.ds(0, PART * 15)]
    pltpu.make_async_copy(others, others, gather_recv).wait()
    whole = pltpu.make_async_remote_copy(
        src_ref=full.at[core], dst_ref=full.at[core], send_sem=whole_send, recv_sem=whole_recv,
        device_id=mate, device_id_type=MESH,
    )
    whole.start()
    for part in range(CHUNKS):
        pass_ring(2, part)
        pass_back(1, part, step_z == 0)
        pass_back(2, part, step_z > 1)
        lift(3, part)
        drop(2, part)
    start_mate_back(0)
    whole.wait()

    square = jnp.zeros((1, 1), F32)
    row_id = lax.broadcasted_iota(jnp.int32, (128, 128), 0)
    col_id = lax.broadcasted_iota(jnp.int32, (128, 128), 1)
    eye = (row_id == col_id).astype(F32)
    upright = [jnp.broadcast_to(average[i : i + 1], (128, 128)).T for i in range(4)]
    for n, (i, j) in enumerate(TILES):
        tile = full[n // 5, pl.ds(128 * (n % 5), 128), :] / TRACKS - upright[i] * average[j : j + 1]
        if i == j:
            tile = tile + EPSILON * eye
        part = jnp.sum(jnp.sum(tile * tile, axis=0, keepdims=True), axis=1, keepdims=True)
        square = square + (part if i == j else 2.0 * part)
        iterate[pl.ds(128 * i, 128), pl.ds(128 * j, 128)] = tile
        if i != j:
            iterate[pl.ds(128 * j, 128), pl.ds(128 * i, 128)] = tile.T
    frobenius = jnp.sqrt(square)
    iterate[...] = iterate[...] / frobenius

    full_row = lax.broadcasted_iota(jnp.int32, (WIDTH, WIDTH), 0)
    full_col = lax.broadcasted_iota(jnp.int32, (WIDTH, WIDTH), 1)
    diagonal = full_row == full_col

    def factor_of(matrix):
        return jnp.where(diagonal, 1.5, 0.0) - 0.5 * matrix

    for sweep in range(NS_ITERS - 1):
        factor = split(factor_of(iterate[...]))
        if sweep == 0:
            inverse[...] = factor_of(iterate[...])
        else:
            inverse[...] = product(split(inverse[...]), factor)
        iterate[...] = product(split(iterate[...]), split(product(factor, factor)))
        if sweep == 1:
            pass_ring(1, 0)
            drop(1, 0)
        if sweep == 2:
            pass_end(3, 0)
    unscaled = product(split(inverse[...]), split(factor_of(iterate[...])))
    whitener[...] = unscaled / jnp.sqrt(frobenius)
    pass_ring(1, 1)
    drop(1, 1)
    weights = split(whitener[...])
    centre = jnp.concatenate([average[i : i + 1] for i in range(4)], axis=1)
    centred = keys[OWN].astype(F32) - centre
    turned = product(split(product(split(centred), weights)), weights)
    queries[...] = (turned * (INV_TEMP / math.sqrt(WIDTH) * math.log2(math.e))).astype(BF16)

    order = [
        BACK, BACK + 1, MATE, used(2), MATE_RING + 2, BACK + 2, MATE + 1,
        used(1), RING, MATE_RING + 1, MATE_RING, MATE + 2,
    ]

    def key_slot(n):
        return sum(jnp.where(n == i, slot, 0) for i, slot in enumerate(order))

    def score(n, high):
        found = lax.dot_general(
            queries[...], keys[key_slot(n)], (((1,), (1,)), ((), ())), preferred_element_type=F32
        )
        found = jnp.where(both(diagonal, n == 0), -jnp.inf, found)
        scores[n] = found
        for i in range(4):
            high = jnp.maximum(high, found[:, 128 * i : 128 * (i + 1)])
        return high

    def attend(state, start, stop):
        before, totals = state
        high = jnp.broadcast_to(before, (ROWS, 128))
        high = lax.fori_loop(start, stop, score, high)
        highest = jnp.max(high, axis=1, keepdims=True)
        if start > 0:
            decay = jnp.exp2(before - highest)
            weighted[...] = weighted[...] * decay
            totals = totals * decay

        def spread(n, totals):
            weight = jnp.exp2(scores[n] - highest).astype(BF16)
            weighted[...] += dot(weight, keys[key_slot(n)])
            wide = weight.astype(F32)
            for i in range(4):
                totals = totals + wide[:, 128 * i : 128 * (i + 1)]
            return totals

        return highest, lax.fori_loop(start, stop, spread, totals)

    pass_end(3, 1)
    for part in range(CHUNKS):
        pass_back(2, part, step_z < 2)
        take_side(3, part)
        take_side(2, part)
    start_mate_back(1)
    start_mate_ring(2)
    each(lambda part: mate_back(0, part).wait_recv())
    weighted[...] = jnp.zeros_like(weighted)
    state = (jnp.full((ROWS, 1), -jnp.inf, F32), jnp.zeros((ROWS, 128), F32))
    state = attend(state, 0, 3)
    each(lambda part: mate_back(1, part).wait_recv())
    each(lambda part: mate_ring(2, part).wait_recv())
    state = attend(state, 3, 7)
    each(lambda part: take_side(1, part))
    start_mate_ring(1)
    when(second, lambda: start_mate_ring(0))
    each(lambda part: take_ring(0, part))
    when(core == 0, lambda: start_mate_ring(0))
    each(lambda part: pass_back(3, part, step_z >= 0))
    start_mate_back(2)
    state = attend(state, 7, 9)
    each(lambda part: mate_ring(1, part).wait_recv())
    each(lambda part: mate_ring(0, part).wait_recv())
    each(lambda part: mate_back(2, part).wait_recv())
    _, totals = attend(state, 9, 12)
    totals = jnp.sum(totals, axis=1, keepdims=True)
    mixed = weighted[...] / totals - centre
    out_ref[...] = product(split(mixed), split(whitener[...])).astype(BF16)

    start_core.wait_send()
    pltpu.make_async_copy(plane_in, plane_in, plane_send).wait()
    pltpu.make_async_copy(line_in, line_in, line_send).wait()
    pltpu.make_async_copy(others, others, gather_send).wait()
    for part in range(CHUNKS):
        for s in range(4):
            ring_hop(s, part).wait_send()
        for i in range(3):
            mate_back(i, part).wait_send()
            mate_ring(i, part).wait_send()
        for s in range(1, 4):
            gone = jnp.logical_or(lower(s), both(last, second) if s == 3 else last)
            when(gone, lambda: side_hop(s, part).wait_send())
        back_hop(1, part).wait_send()
        back_hop(2, part).wait_send()
        when(second, lambda: back_hop(3, part).wait_send())


def local(tracks):
    dma = pltpu.SemaphoreType.DMA
    return pl.pallas_call(
        kernel,
        out_shape=jax.ShapeDtypeStruct((ROWS, WIDTH), BF16),
        in_specs=[pl.BlockSpec(memory_space=pl.ANY)],
        out_specs=pl.BlockSpec(memory_space=pltpu.VMEM),
        scratch_shapes=[
            pltpu.VMEM((SLOTS, ROWS, WIDTH), BF16),
            pltpu.VMEM((2, HALF + 8, 128), F32),
            pltpu.VMEM((HALF + 8, 128), F32),
            pltpu.VMEM((16, PART + 8, 128), F32),
            pltpu.VMEM((15, PART + 8, 128), F32),
            pltpu.VMEM((PART + 8, 128), F32),
            pltpu.VMEM((7, PART + 8, 128), F32),
            pltpu.VMEM((2, HALF, 128), F32),
            pltpu.VMEM((WIDTH, WIDTH), F32),
            pltpu.VMEM((WIDTH, WIDTH), F32),
            pltpu.VMEM((12, ROWS, ROWS), F32),
            pltpu.VMEM((ROWS, WIDTH), F32),
            pltpu.VMEM((ROWS, WIDTH), BF16),
            pltpu.VMEM((WIDTH, WIDTH), F32),
            dma(()),
            dma((4, CHUNKS)), dma((4, CHUNKS)),
            dma((4, CHUNKS)), dma((4, CHUNKS)),
            dma((4, CHUNKS)), dma((4, CHUNKS)),
            dma((6, CHUNKS)), dma((6, CHUNKS)),
            dma(()), dma(()), dma(()), dma(()), dma(()), dma(()), dma(()), dma(()), dma(()), dma(()),
        ],
        compiler_params=pltpu.CompilerParams(
            collective_id=0, has_side_effects=True, vmem_limit_bytes=56 * 1024 * 1024
        ),
    )(tracks)


def solution(mesh):
    spec = P(("blk", "rep"), None)
    return jax.shard_map(local, mesh=mesh, in_specs=(spec,), out_specs=spec, check_vma=False)
```

```python
import functools
import math

import jax
import jax.numpy as jnp
from jax import lax
from jax.experimental import pallas as pl
from jax.experimental.pallas import tpu as pltpu
from jax.sharding import PartitionSpec as P

NS_ITERS = 4
INV_TEMP = 2
EPSILON = 1e-05
WIDTH = 512
ROWS = 512
TRACKS = 131072
MESH = pl.DeviceIdType.MESH
F32 = jnp.float32
BF16 = jnp.bfloat16

TILES = [(i, j) for i in range(4) for j in range(i, 4)]
HALF = 640
PART = 40
PLANE = [(dy, dx) for dy in range(4) for dx in range(4)][1:]

OWN, BACK, RING, SIDE, MATE, MATE_RING = 0, 0, 4, 8, 12, 15
SLOTS = 18
CHUNKS = 2
CHUNK = ROWS // CHUNKS


def place(y, x, z, core):
    return (((y * 4 + x) * 4 + z % 4) * 2 + core, z // 4)


def split(value):
    high = value.astype(BF16)
    return high, (value - high.astype(F32)).astype(BF16)


def dot(left, right):
    return jnp.dot(left, right, preferred_element_type=F32)


def product(left, right):
    wide = jnp.concatenate([left[0], left[0], left[1]], axis=1)
    return dot(wide, jnp.concatenate([right[0], right[1], right[0]], axis=0))


def kernel(
    tracks_ref, out_ref, keys, halves, from_mate, outgoing, plane_in, line_out, line_in, full,
    iterate, inverse, scores, weighted, queries, whitener, load_sem, ring_send, ring_recv,
    back_send, back_recv, side_send, side_recv, mate_send, mate_recv, core_send, core_recv,
    plane_send, plane_recv, line_send, line_recv, gather_send, gather_recv, whole_send, whole_recv,
):
    group = lax.axis_index("blk")
    rep = lax.axis_index("rep")
    y, x, core = group // 32, (group // 8) % 4, group % 2
    step_z = (group // 2) % 4
    z = rep * 4 + step_z
    mine = y * 4 + x
    wrap = (x + 1) // 4
    next_y, next_x = (y + wrap) % 4, (x + 1) % 4
    mate = place(y, x, z, 1 - core)
    down = place(y, x, (z + 7) % 8, core)
    column = place(next_y, next_x, z, core)
    up = place(y, x, (z + 1) % 8, core)
    at_end = (step_z + 1) // 4

    load = pltpu.make_async_copy(tracks_ref, keys.at[OWN], load_sem)
    load.start()
    barrier = pltpu.get_barrier_semaphore()

    def greet(device):
        pl.semaphore_signal(barrier, inc=1, device_id=device, device_id_type=MESH)

    greet(mate)
    for dz in range(1, 8):
        greet(place(y, x, (z + dz) % 8, core))
    for dy, dx in PLANE:
        greet(place((y + dy) % 4, (x + dx) % 4, z, core))

    load.wait()

    rows = keys[OWN]
    gram = lax.dot_general(rows, rows, (((0,), (0,)), ((), ())), preferred_element_type=F32)
    for n, (i, j) in enumerate(TILES):
        halves[n // 5, pl.ds(128 * (n % 5), 128), :] = gram[
            128 * i : 128 * (i + 1), 128 * j : 128 * (j + 1)
        ]
    sums = jnp.sum(rows.astype(F32), axis=0, keepdims=True)
    tail = jnp.concatenate(
        [sums[:, 128 * i : 128 * (i + 1)] for i in range(4)] + [jnp.zeros((4, 128), F32)], axis=0
    )
    for h in range(2):
        halves[h, pl.ds(HALF, 8), :] = tail

    pl.semaphore_wait(barrier, 23)

    def piece(slot, part):
        return keys.at[slot, pl.ds(part * CHUNK, CHUNK)]

    def mover(source, target, part, send, recv, device):
        return pltpu.make_async_remote_copy(
            src_ref=piece(source, part),
            dst_ref=piece(target, part),
            send_sem=send,
            recv_sem=recv,
            device_id=device,
            device_id_type=MESH,
        )

    def ring_hop(s, part):
        source = OWN if s == 3 else RING + s + 1
        return mover(
            source, RING + s, part, ring_send.at[s, part], ring_recv.at[s, part], down
        )

    def back_hop(s, part):
        source = BACK + s - 1 + at_end * (SIDE - BACK + 1)
        return mover(
            source, BACK + s, part, back_send.at[s, part], back_recv.at[s, part], up
        )

    def side_hop(s, part):
        source = RING + s + at_end * (BACK - 1 - RING)
        return mover(
            source, SIDE + s, part, side_send.at[s, part], side_recv.at[s, part], column
        )

    def used(s):
        return RING + s + 4 * jnp.minimum(jnp.maximum(s - step_z, 0), 1)

    def mate_back(i, part):
        return mover(
            BACK + core + i, MATE + i, part, mate_send.at[i, part], mate_recv.at[i, part], mate
        )

    def mate_ring(i, part):
        return mover(
            used(core + i), MATE_RING + i, part,
            mate_send.at[3 + i, part], mate_recv.at[3 + i, part], mate,
        )

    def each(act):
        for part in range(CHUNKS):
            act(part)

    def start_mate_back(i):
        each(lambda part: mate_back(i, part).start())

    def start_mate_ring(i):
        each(lambda part: mate_ring(i, part).start())

    def when(cond, act):
        @pl.when(cond)
        def _():
            act()

    inner = step_z < 3
    last = step_z == 3
    second = core == 1

    both = jnp.logical_and

    def lower(s):
        return both(step_z < s, second) if s == 3 else step_z < s

    def start_own(part):
        ring_hop(3, part).start()
        when(inner, lambda: back_hop(1, part).start())

    def take_ring(s, part):
        ring_hop(s, part).wait_recv()

    def send_ring(s, part):
        ring_hop(s - 1, part).start()

    def pass_ring(s, part):
        take_ring(s, part)
        send_ring(s, part)

    def drop(s, part):
        when(lower(s), lambda: side_hop(s, part).start())

    def lift(s, part):
        when(both(last, second) if s == 3 else last, lambda: side_hop(s, part).start())

    def pass_end(s, part):
        def go():
            side_hop(s, part).wait_recv()
            back_hop(s, part).start()

        when(both(last, second) if s == 3 else last, go)

    def pass_back(s, part, here):
        def go():
            back_hop(s, part).wait_recv()
            if s < 3:
                sends = both(inner, second) if s == 2 else inner
                when(sends, lambda: back_hop(s + 1, part).start())

        when(both(here, second) if s == 3 else here, go)

    def take_side(s, part):
        when(lower(s), lambda: side_hop(s, part).wait_recv())

    start_core = pltpu.make_async_remote_copy(
        src_ref=halves.at[1 - core], dst_ref=from_mate, send_sem=core_send, recv_sem=core_recv,
        device_id=mate, device_id_type=MESH,
    )
    start_core.start()
    each(start_own)
    start_core.wait_recv()
    chip = halves[core] + from_mate[...]
    for q in range(16):
        outgoing[q, pl.ds(0, PART), :] = chip[PART * q : PART * (q + 1)]
        outgoing[q, pl.ds(PART, 8), :] = chip[HALF : HALF + 8]

    def plane_hop(n, dy, dx):
        ty, tx = (y + dy) % 4, (x + dx) % 4
        return pltpu.make_async_remote_copy(
            src_ref=outgoing.at[ty * 4 + tx], dst_ref=plane_in.at[n], send_sem=plane_send,
            recv_sem=plane_recv, device_id=place(ty, tx, z, core), device_id_type=MESH,
        )

    for n, (dy, dx) in enumerate(PLANE):
        plane_hop(n, dy, dx).start()
    each(lambda part: lift(1, part))
    pltpu.make_async_copy(plane_in, plane_in, plane_recv).wait()
    line_out[...] = outgoing[mine] + jnp.sum(plane_in[...], axis=0)

    def line_hop(dz):
        return pltpu.make_async_remote_copy(
            src_ref=line_out, dst_ref=line_in.at[dz - 1], send_sem=line_send, recv_sem=line_recv,
            device_id=place(y, x, (z + dz) % 8, core), device_id_type=MESH,
        )

    for dz in range(1, 8):
        line_hop(dz).start()
    for part in range(CHUNKS):
        pass_back(1, part, last)
        lift(2, part)
        take_ring(3, part)
        if part == 0:
            send_ring(3, part)
            pass_end(1, part)
            pass_back(1, part, both(step_z > 0, inner))
        drop(3, part)
    pltpu.make_async_copy(line_in, line_in, line_recv).wait()
    total = line_out[...] + jnp.sum(line_in[...], axis=0)
    full[core, pl.ds(pl.multiple_of(PART * mine, 8), PART), :] = total[:PART]
    average = total[PART : PART + 4] / TRACKS

    def gather_hop(dy, dx):
        area = full.at[core, pl.ds(pl.multiple_of(PART * mine, 8), PART)]
        return pltpu.make_async_remote_copy(
            src_ref=area, dst_ref=area, send_sem=gather_send, recv_sem=gather_recv,
            device_id=place((y + dy) % 4, (x + dx) % 4, z, core), device_id_type=MESH,
        )

    for dy, dx in PLANE:
        gather_hop(dy, dx).start()
    for part in range(1, CHUNKS):
        send_ring(3, part)
        pass_end(1, part)
        pass_back(1, part, both(step_z > 0, inner))
    pass_ring(2, 0)
    drop(2, 0)
    each(lambda part: pass_end(2, part))
    pass_back(1, 0, step_z == 0)
    pass_back(2, 0, step_z > 1)
    lift(3, 0)
    others = full.at[core, pl.ds(0, PART * 15)]
    pltpu.make_async_copy(others, others, gather_recv).wait()
    whole = pltpu.make_async_remote_copy(
        src_ref=full.at[core], dst_ref=full.at[core], send_sem=whole_send, recv_sem=whole_recv,
        device_id=mate, device_id_type=MESH,
    )
    whole.start()
    for part in range(1, CHUNKS):
        pass_ring(2, part)
        pass_back(1, part, step_z == 0)
        pass_back(2, part, step_z > 1)
        lift(3, part)
        drop(2, part)
    start_mate_back(0)
    whole.wait()

    square = jnp.zeros((1, 1), F32)
    row_id = lax.broadcasted_iota(jnp.int32, (128, 128), 0)
    col_id = lax.broadcasted_iota(jnp.int32, (128, 128), 1)
    eye = (row_id == col_id).astype(F32)
    upright = [jnp.broadcast_to(average[i : i + 1], (128, 128)).T for i in range(4)]
    for n, (i, j) in enumerate(TILES):
        tile = full[n // 5, pl.ds(128 * (n % 5), 128), :] / TRACKS - upright[i] * average[j : j + 1]
        if i == j:
            tile = tile + EPSILON * eye
        part = jnp.sum(jnp.sum(tile * tile, axis=0, keepdims=True), axis=1, keepdims=True)
        square = square + (part if i == j else 2.0 * part)
        iterate[pl.ds(128 * i, 128), pl.ds(128 * j, 128)] = tile
        if i != j:
            iterate[pl.ds(128 * j, 128), pl.ds(128 * i, 128)] = tile.T
    frobenius = jnp.sqrt(square)
    iterate[...] = iterate[...] / frobenius

    full_row = lax.broadcasted_iota(jnp.int32, (WIDTH, WIDTH), 0)
    full_col = lax.broadcasted_iota(jnp.int32, (WIDTH, WIDTH), 1)
    diagonal = full_row == full_col

    def factor_of(matrix):
        return jnp.where(diagonal, 1.5, 0.0) - 0.5 * matrix

    for sweep in range(NS_ITERS - 1):
        factor = split(factor_of(iterate[...]))
        if sweep == 0:
            inverse[...] = factor_of(iterate[...])
        else:
            inverse[...] = product(split(inverse[...]), factor)
        iterate[...] = product(split(iterate[...]), split(product(factor, factor)))
        if sweep == 0:
            pass_ring(1, 0)
            drop(1, 0)
            pass_end(3, 0)
        if sweep == 1:
            pass_ring(1, 1)
            drop(1, 1)
            pass_back(2, 0, step_z < 2)
        if sweep == 2:
            pass_end(3, 1)
            pass_back(2, 1, step_z < 2)
    unscaled = product(split(inverse[...]), split(factor_of(iterate[...])))
    whitener[...] = unscaled / jnp.sqrt(frobenius)
    weights = split(whitener[...])
    centre = jnp.concatenate([average[i : i + 1] for i in range(4)], axis=1)
    centred = keys[OWN].astype(F32) - centre
    turned = product(split(product(split(centred), weights)), weights)
    queries[...] = (turned * (INV_TEMP / math.sqrt(WIDTH) * math.log2(math.e))).astype(BF16)

    order = [
        BACK, BACK + 1, MATE, used(2), MATE_RING + 2, BACK + 2, MATE + 1,
        used(1), RING, MATE_RING + 1, MATE_RING, MATE + 2,
    ]

    def key_slot(n):
        return order[n]

    def score(n, high, own=False):
        found = lax.dot_general(
            queries[...], keys[key_slot(n)], (((1,), (1,)), ((), ())), preferred_element_type=F32
        )
        if own:
            found = jnp.where(diagonal, -jnp.inf, found)
        scores[n] = found
        for i in range(4):
            high = jnp.maximum(high, found[:, 128 * i : 128 * (i + 1)])
        return high

    def attend(state, start, stop):
        before, totals = state
        high = jnp.broadcast_to(before, (ROWS, 128))
        if start == 0:
            high = score(0, high, True)
        for n in range(max(start, 1), stop):
            high = score(n, high)
        highest = jnp.max(high, axis=1, keepdims=True)
        if start > 0:
            decay = jnp.exp2(before - highest)
            weighted[...] = weighted[...] * decay
            totals = totals * decay

        def spread(n, totals):
            weight = jnp.exp2(scores[n] - highest).astype(BF16)
            weighted[...] += dot(weight, keys[key_slot(n)])
            wide = weight.astype(F32)
            for i in range(4):
                totals = totals + wide[:, 128 * i : 128 * (i + 1)]
            return totals

        for n in range(start, stop):
            totals = spread(n, totals)
        return highest, totals

    for part in range(CHUNKS):
        take_side(3, part)
        take_side(2, part)
    start_mate_back(1)
    start_mate_ring(2)
    each(lambda part: mate_back(0, part).wait_recv())
    weighted[...] = jnp.zeros_like(weighted)
    state = (jnp.full((ROWS, 1), -jnp.inf, F32), jnp.zeros((ROWS, 128), F32))
    state = attend(state, 0, 3)
    each(lambda part: mate_back(1, part).wait_recv())
    each(lambda part: mate_ring(2, part).wait_recv())
    state = attend(state, 3, 7)
    each(lambda part: take_side(1, part))
    start_mate_ring(1)
    when(second, lambda: start_mate_ring(0))
    each(lambda part: take_ring(0, part))
    when(core == 0, lambda: start_mate_ring(0))
    each(lambda part: pass_back(3, part, step_z >= 0))
    start_mate_back(2)
    state = attend(state, 7, 9)
    each(lambda part: mate_ring(1, part).wait_recv())
    each(lambda part: mate_ring(0, part).wait_recv())
    each(lambda part: mate_back(2, part).wait_recv())
    _, totals = attend(state, 9, 12)
    totals = jnp.sum(totals, axis=1, keepdims=True)
    mixed = weighted[...] / totals - centre
    out_ref[...] = product(split(mixed), split(whitener[...])).astype(BF16)

    start_core.wait_send()
    pltpu.make_async_copy(plane_in, plane_in, plane_send).wait()
    pltpu.make_async_copy(line_in, line_in, line_send).wait()
    pltpu.make_async_copy(others, others, gather_send).wait()
    for part in range(CHUNKS):
        for s in range(4):
            ring_hop(s, part).wait_send()
        for i in range(3):
            mate_back(i, part).wait_send()
            mate_ring(i, part).wait_send()
        for s in range(1, 4):
            gone = jnp.logical_or(lower(s), both(last, second) if s == 3 else last)
            when(gone, lambda: side_hop(s, part).wait_send())
        back_hop(1, part).wait_send()
        back_hop(2, part).wait_send()
        when(second, lambda: back_hop(3, part).wait_send())


def local(tracks):
    dma = pltpu.SemaphoreType.DMA
    return pl.pallas_call(
        kernel,
        out_shape=jax.ShapeDtypeStruct((ROWS, WIDTH), BF16),
        in_specs=[pl.BlockSpec(memory_space=pl.ANY)],
        out_specs=pl.BlockSpec(memory_space=pltpu.VMEM),
        scratch_shapes=[
            pltpu.VMEM((SLOTS, ROWS, WIDTH), BF16),
            pltpu.VMEM((2, HALF + 8, 128), F32),
            pltpu.VMEM((HALF + 8, 128), F32),
            pltpu.VMEM((16, PART + 8, 128), F32),
            pltpu.VMEM((15, PART + 8, 128), F32),
            pltpu.VMEM((PART + 8, 128), F32),
            pltpu.VMEM((7, PART + 8, 128), F32),
            pltpu.VMEM((2, HALF, 128), F32),
            pltpu.VMEM((WIDTH, WIDTH), F32),
            pltpu.VMEM((WIDTH, WIDTH), F32),
            pltpu.VMEM((12, ROWS, ROWS), F32),
            pltpu.VMEM((ROWS, WIDTH), F32),
            pltpu.VMEM((ROWS, WIDTH), BF16),
            pltpu.VMEM((WIDTH, WIDTH), F32),
            dma(()),
            dma((4, CHUNKS)), dma((4, CHUNKS)),
            dma((4, CHUNKS)), dma((4, CHUNKS)),
            dma((4, CHUNKS)), dma((4, CHUNKS)),
            dma((6, CHUNKS)), dma((6, CHUNKS)),
            dma(()), dma(()), dma(()), dma(()), dma(()), dma(()), dma(()), dma(()), dma(()), dma(()),
        ],
        compiler_params=pltpu.CompilerParams(
            collective_id=0, has_side_effects=True, vmem_limit_bytes=56 * 1024 * 1024
        ),
    )(tracks)


def solution(mesh):
    spec = P(("blk", "rep"), None)
    return jax.shard_map(local, mesh=mesh, in_specs=(spec,), out_specs=spec, check_vma=False)
```

```python
import functools
import math

import jax
import jax.numpy as jnp
from jax import lax
from jax.experimental import pallas as pl
from jax.experimental.pallas import tpu as pltpu
from jax.sharding import PartitionSpec as P

NS_ITERS = 4
INV_TEMP = 2
EPSILON = 1e-05
WIDTH = 512
ROWS = 512
TRACKS = 131072
MESH = pl.DeviceIdType.MESH
F32 = jnp.float32
BF16 = jnp.bfloat16

TILES = [(i, j) for i in range(4) for j in range(i, 4)]
HALF = 640
PART = 40
PLANE = [(dy, dx) for dy in range(4) for dx in range(4)][1:]

OWN, BACK, RING, SIDE, MATE, MATE_RING = 0, 0, 4, 8, 12, 15
SLOTS = 18
CHUNKS = 2
CHUNK = ROWS // CHUNKS


def place(y, x, z, core):
    return (((y * 4 + x) * 4 + z % 4) * 2 + core, z // 4)


def split(value):
    high = value.astype(BF16)
    return high, (value - high.astype(F32)).astype(BF16)


def dot(left, right):
    return jnp.dot(left, right, preferred_element_type=F32)


def product(left, right):
    wide = jnp.concatenate([left[0], left[0], left[1]], axis=1)
    return dot(wide, jnp.concatenate([right[0], right[1], right[0]], axis=0))


def kernel(
    tracks_ref, out_ref, keys, halves, from_mate, outgoing, plane_in, line_out, line_in, full,
    iterate, inverse, scores, weighted, queries, whitener, load_sem, ring_send, ring_recv,
    back_send, back_recv, side_send, side_recv, mate_send, mate_recv, core_send, core_recv,
    plane_send, plane_recv, line_send, line_recv, gather_send, gather_recv, whole_send, whole_recv,
):
    group = lax.axis_index("blk")
    rep = lax.axis_index("rep")
    y, x, core = group // 32, (group // 8) % 4, group % 2
    step_z = (group // 2) % 4
    z = rep * 4 + step_z
    mine = y * 4 + x
    wrap = (x + 1) // 4
    next_y, next_x = (y + wrap) % 4, (x + 1) % 4
    mate = place(y, x, z, 1 - core)
    down = place(y, x, (z + 7) % 8, core)
    column = place(next_y, next_x, z, core)
    up = place(y, x, (z + 1) % 8, core)
    at_end = (step_z + 1) // 4

    load = pltpu.make_async_copy(tracks_ref, keys.at[OWN], load_sem)
    load.start()
    barrier = pltpu.get_barrier_semaphore()

    def greet(device):
        pl.semaphore_signal(barrier, inc=1, device_id=device, device_id_type=MESH)

    greet(mate)
    for dz in range(1, 8):
        greet(place(y, x, (z + dz) % 8, core))
    for dy, dx in PLANE:
        greet(place((y + dy) % 4, (x + dx) % 4, z, core))

    load.wait()

    rows = keys[OWN]
    gram = lax.dot_general(rows, rows, (((0,), (0,)), ((), ())), preferred_element_type=F32)
    for n, (i, j) in enumerate(TILES):
        halves[n // 5, pl.ds(128 * (n % 5), 128), :] = gram[
            128 * i : 128 * (i + 1), 128 * j : 128 * (j + 1)
        ]
    sums = jnp.sum(rows.astype(F32), axis=0, keepdims=True)
    tail = jnp.concatenate(
        [sums[:, 128 * i : 128 * (i + 1)] for i in range(4)] + [jnp.zeros((4, 128), F32)], axis=0
    )
    for h in range(2):
        halves[h, pl.ds(HALF, 8), :] = tail

    pl.semaphore_wait(barrier, 23)

    def piece(slot, part):
        return keys.at[slot, pl.ds(part * CHUNK, CHUNK)]

    def mover(source, target, part, send, recv, device):
        return pltpu.make_async_remote_copy(
            src_ref=piece(source, part),
            dst_ref=piece(target, part),
            send_sem=send,
            recv_sem=recv,
            device_id=device,
            device_id_type=MESH,
        )

    def ring_hop(s, part):
        source = OWN if s == 3 else RING + s + 1
        return mover(
            source, RING + s, part, ring_send.at[s, part], ring_recv.at[s, part], down
        )

    def back_hop(s, part):
        source = BACK + s - 1 + at_end * (SIDE - BACK + 1)
        return mover(
            source, BACK + s, part, back_send.at[s, part], back_recv.at[s, part], up
        )

    def side_hop(s, part):
        source = RING + s + at_end * (BACK - 1 - RING)
        return mover(
            source, SIDE + s, part, side_send.at[s, part], side_recv.at[s, part], column
        )

    def used(s):
        return RING + s + 4 * jnp.minimum(jnp.maximum(s - step_z, 0), 1)

    def mate_back(i, part):
        return mover(
            BACK + core + i, MATE + i, part, mate_send.at[i, part], mate_recv.at[i, part], mate
        )

    def mate_ring(i, part):
        return mover(
            used(core + i), MATE_RING + i, part,
            mate_send.at[3 + i, part], mate_recv.at[3 + i, part], mate,
        )

    def each(act):
        for part in range(CHUNKS):
            act(part)

    def start_mate_back(i):
        each(lambda part: mate_back(i, part).start())

    def start_mate_ring(i):
        each(lambda part: mate_ring(i, part).start())

    def when(cond, act):
        @pl.when(cond)
        def _():
            act()

    inner = step_z < 3
    last = step_z == 3
    second = core == 1

    both = jnp.logical_and

    def lower(s):
        return both(step_z < s, second) if s == 3 else step_z < s

    def start_own(part):
        ring_hop(3, part).start()
        when(inner, lambda: back_hop(1, part).start())

    def take_ring(s, part):
        ring_hop(s, part).wait_recv()

    def send_ring(s, part):
        ring_hop(s - 1, part).start()

    def pass_ring(s, part):
        take_ring(s, part)
        send_ring(s, part)

    def drop(s, part):
        when(lower(s), lambda: side_hop(s, part).start())

    def lift(s, part):
        when(both(last, second) if s == 3 else last, lambda: side_hop(s, part).start())

    def pass_end(s, part):
        def go():
            side_hop(s, part).wait_recv()
            back_hop(s, part).start()

        when(both(last, second) if s == 3 else last, go)

    def pass_back(s, part, here):
        def go():
            back_hop(s, part).wait_recv()
            if s < 3:
                sends = both(inner, second) if s == 2 else inner
                when(sends, lambda: back_hop(s + 1, part).start())

        when(both(here, second) if s == 3 else here, go)

    def take_side(s, part):
        when(lower(s), lambda: side_hop(s, part).wait_recv())

    start_core = pltpu.make_async_remote_copy(
        src_ref=halves.at[1 - core], dst_ref=from_mate, send_sem=core_send, recv_sem=core_recv,
        device_id=mate, device_id_type=MESH,
    )
    start_core.start()
    each(start_own)
    start_core.wait_recv()
    chip = halves[core] + from_mate[...]
    for q in range(16):
        outgoing[q, pl.ds(0, PART), :] = chip[PART * q : PART * (q + 1)]
        outgoing[q, pl.ds(PART, 8), :] = chip[HALF : HALF + 8]

    def plane_hop(n, dy, dx):
        ty, tx = (y + dy) % 4, (x + dx) % 4
        return pltpu.make_async_remote_copy(
            src_ref=outgoing.at[ty * 4 + tx], dst_ref=plane_in.at[n], send_sem=plane_send,
            recv_sem=plane_recv, device_id=place(ty, tx, z, core), device_id_type=MESH,
        )

    for n, (dy, dx) in enumerate(PLANE):
        plane_hop(n, dy, dx).start()
    each(lambda part: lift(1, part))
    pltpu.make_async_copy(plane_in, plane_in, plane_recv).wait()
    line_out[...] = outgoing[mine] + jnp.sum(plane_in[...], axis=0)

    def line_hop(dz):
        return pltpu.make_async_remote_copy(
            src_ref=line_out, dst_ref=line_in.at[dz - 1], send_sem=line_send, recv_sem=line_recv,
            device_id=place(y, x, (z + dz) % 8, core), device_id_type=MESH,
        )

    for dz in range(1, 8):
        line_hop(dz).start()
    for part in range(CHUNKS):
        pass_back(1, part, last)
        lift(2, part)
        take_ring(3, part)
        if part == 0:
            send_ring(3, part)
            pass_end(1, part)
            pass_back(1, part, both(step_z > 0, inner))
        drop(3, part)
    pltpu.make_async_copy(line_in, line_in, line_recv).wait()
    total = line_out[...] + jnp.sum(line_in[...], axis=0)
    full[core, pl.ds(pl.multiple_of(PART * mine, 8), PART), :] = total[:PART]
    average = total[PART : PART + 4] / TRACKS

    def gather_hop(dy, dx):
        area = full.at[core, pl.ds(pl.multiple_of(PART * mine, 8), PART)]
        return pltpu.make_async_remote_copy(
            src_ref=area, dst_ref=area, send_sem=gather_send, recv_sem=gather_recv,
            device_id=place((y + dy) % 4, (x + dx) % 4, z, core), device_id_type=MESH,
        )

    for dy, dx in PLANE:
        gather_hop(dy, dx).start()
    for part in range(1, CHUNKS):
        send_ring(3, part)
        pass_end(1, part)
        pass_back(1, part, both(step_z > 0, inner))
    pass_ring(2, 0)
    drop(2, 0)
    each(lambda part: pass_end(2, part))
    pass_back(1, 0, step_z == 0)
    pass_back(2, 0, step_z > 1)
    lift(3, 0)
    for part in range(1, CHUNKS):
        pass_ring(2, part)
        pass_back(1, part, step_z == 0)
        pass_back(2, part, step_z > 1)
        lift(3, part)
        drop(2, part)
    others = full.at[core, pl.ds(0, PART * 15)]
    pltpu.make_async_copy(others, others, gather_recv).wait()
    whole = pltpu.make_async_remote_copy(
        src_ref=full.at[core], dst_ref=full.at[core], send_sem=whole_send, recv_sem=whole_recv,
        device_id=mate, device_id_type=MESH,
    )
    whole.start()
    pass_ring(1, 0)
    drop(1, 0)
    start_mate_back(0)
    whole.wait()

    square = jnp.zeros((1, 1), F32)
    row_id = lax.broadcasted_iota(jnp.int32, (128, 128), 0)
    col_id = lax.broadcasted_iota(jnp.int32, (128, 128), 1)
    eye = (row_id == col_id).astype(F32)
    upright = [jnp.broadcast_to(average[i : i + 1], (128, 128)).T for i in range(4)]
    for n, (i, j) in enumerate(TILES):
        tile = full[n // 5, pl.ds(128 * (n % 5), 128), :] / TRACKS - upright[i] * average[j : j + 1]
        if i == j:
            tile = tile + EPSILON * eye
        part = jnp.sum(jnp.sum(tile * tile, axis=0, keepdims=True), axis=1, keepdims=True)
        square = square + (part if i == j else 2.0 * part)
        iterate[pl.ds(128 * i, 128), pl.ds(128 * j, 128)] = tile
        if i != j:
            iterate[pl.ds(128 * j, 128), pl.ds(128 * i, 128)] = tile.T
    frobenius = jnp.sqrt(square)
    iterate[...] = iterate[...] / frobenius

    full_row = lax.broadcasted_iota(jnp.int32, (WIDTH, WIDTH), 0)
    full_col = lax.broadcasted_iota(jnp.int32, (WIDTH, WIDTH), 1)
    diagonal = full_row == full_col

    def factor_of(matrix):
        return jnp.where(diagonal, 1.5, 0.0) - 0.5 * matrix

    for sweep in range(NS_ITERS - 1):
        factor = split(factor_of(iterate[...]))
        if sweep == 0:
            inverse[...] = factor_of(iterate[...])
        else:
            inverse[...] = product(split(inverse[...]), factor)
        iterate[...] = product(split(iterate[...]), split(product(factor, factor)))
        if sweep == 0:
            pass_end(3, 0)
            pass_ring(1, 1)
            drop(1, 1)
        if sweep == 1:
            pass_back(2, 0, step_z < 2)
            pass_end(3, 1)
        if sweep == 2:
            pass_back(2, 1, step_z < 2)
            for part in range(CHUNKS):
                take_side(3, part)
                take_side(2, part)
            start_mate_back(1)
            start_mate_ring(2)
    unscaled = product(split(inverse[...]), split(factor_of(iterate[...])))
    whitener[...] = unscaled / jnp.sqrt(frobenius)
    weights = split(whitener[...])
    centre = jnp.concatenate([average[i : i + 1] for i in range(4)], axis=1)
    centred = keys[OWN].astype(F32) - centre
    turned = product(split(product(split(centred), weights)), weights)
    queries[...] = (turned * (INV_TEMP / math.sqrt(WIDTH) * math.log2(math.e))).astype(BF16)

    order = [
        BACK, BACK + 1, MATE, used(2), MATE_RING + 2, BACK + 2, MATE + 1,
        used(1), RING, MATE_RING + 1, MATE_RING, MATE + 2,
    ]

    def key_slot(n):
        return order[n]

    def score(n, high, own=False):
        found = lax.dot_general(
            queries[...], keys[key_slot(n)], (((1,), (1,)), ((), ())), preferred_element_type=F32
        )
        if own:
            found = jnp.where(diagonal, -jnp.inf, found)
        scores[n] = found
        for i in range(4):
            high = jnp.maximum(high, found[:, 128 * i : 128 * (i + 1)])
        return high

    def attend(state, start, stop):
        before, totals = state
        high = jnp.broadcast_to(before, (ROWS, 128))
        if start == 0:
            high = score(0, high, True)
        for n in range(max(start, 1), stop):
            high = score(n, high)
        highest = jnp.max(high, axis=1, keepdims=True)
        if start > 0:
            decay = jnp.exp2(before - highest)
            weighted[...] = weighted[...] * decay
            totals = totals * decay

        def spread(n, totals):
            weight = jnp.exp2(scores[n] - highest).astype(BF16)
            weighted[...] += dot(weight, keys[key_slot(n)])
            wide = weight.astype(F32)
            for i in range(4):
                totals = totals + wide[:, 128 * i : 128 * (i + 1)]
            return totals

        for n in range(start, stop):
            totals = spread(n, totals)
        return highest, totals

    each(lambda part: mate_back(0, part).wait_recv())
    weighted[...] = jnp.zeros_like(weighted)
    state = (jnp.full((ROWS, 1), -jnp.inf, F32), jnp.zeros((ROWS, 128), F32))
    state = attend(state, 0, 3)
    each(lambda part: mate_back(1, part).wait_recv())
    each(lambda part: mate_ring(2, part).wait_recv())
    each(lambda part: take_side(1, part))
    start_mate_ring(1)
    when(second, lambda: start_mate_ring(0))
    state = attend(state, 3, 7)
    each(lambda part: take_ring(0, part))
    when(core == 0, lambda: start_mate_ring(0))
    each(lambda part: pass_back(3, part, step_z >= 0))
    start_mate_back(2)
    state = attend(state, 7, 9)
    each(lambda part: mate_ring(1, part).wait_recv())
    each(lambda part: mate_ring(0, part).wait_recv())
    each(lambda part: mate_back(2, part).wait_recv())
    _, totals = attend(state, 9, 12)
    totals = jnp.sum(totals, axis=1, keepdims=True)
    mixed = weighted[...] / totals - centre
    out_ref[...] = product(split(mixed), split(whitener[...])).astype(BF16)

    start_core.wait_send()
    pltpu.make_async_copy(plane_in, plane_in, plane_send).wait()
    pltpu.make_async_copy(line_in, line_in, line_send).wait()
    pltpu.make_async_copy(others, others, gather_send).wait()
    for part in range(CHUNKS):
        for s in range(4):
            ring_hop(s, part).wait_send()
        for i in range(3):
            mate_back(i, part).wait_send()
            mate_ring(i, part).wait_send()
        for s in range(1, 4):
            gone = jnp.logical_or(lower(s), both(last, second) if s == 3 else last)
            when(gone, lambda: side_hop(s, part).wait_send())
        back_hop(1, part).wait_send()
        back_hop(2, part).wait_send()
        when(second, lambda: back_hop(3, part).wait_send())


def local(tracks):
    dma = pltpu.SemaphoreType.DMA
    return pl.pallas_call(
        kernel,
        out_shape=jax.ShapeDtypeStruct((ROWS, WIDTH), BF16),
        in_specs=[pl.BlockSpec(memory_space=pl.ANY)],
        out_specs=pl.BlockSpec(memory_space=pltpu.VMEM),
        scratch_shapes=[
            pltpu.VMEM((SLOTS, ROWS, WIDTH), BF16),
            pltpu.VMEM((2, HALF + 8, 128), F32),
            pltpu.VMEM((HALF + 8, 128), F32),
            pltpu.VMEM((16, PART + 8, 128), F32),
            pltpu.VMEM((15, PART + 8, 128), F32),
            pltpu.VMEM((PART + 8, 128), F32),
            pltpu.VMEM((7, PART + 8, 128), F32),
            pltpu.VMEM((2, HALF, 128), F32),
            pltpu.VMEM((WIDTH, WIDTH), F32),
            pltpu.VMEM((WIDTH, WIDTH), F32),
            pltpu.VMEM((12, ROWS, ROWS), F32),
            pltpu.VMEM((ROWS, WIDTH), F32),
            pltpu.VMEM((ROWS, WIDTH), BF16),
            pltpu.VMEM((WIDTH, WIDTH), F32),
            dma(()),
            dma((4, CHUNKS)), dma((4, CHUNKS)),
            dma((4, CHUNKS)), dma((4, CHUNKS)),
            dma((4, CHUNKS)), dma((4, CHUNKS)),
            dma((6, CHUNKS)), dma((6, CHUNKS)),
            dma(()), dma(()), dma(()), dma(()), dma(()), dma(()), dma(()), dma(()), dma(()), dma(()),
        ],
        compiler_params=pltpu.CompilerParams(
            collective_id=0, has_side_effects=True, vmem_limit_bytes=56 * 1024 * 1024
        ),
    )(tracks)


def solution(mesh):
    spec = P(("blk", "rep"), None)
    return jax.shard_map(local, mesh=mesh, in_specs=(spec,), out_specs=spec, check_vma=False)
```
